32 devices in a mesh: row: 8 (over y, x, core), col: 4 (over z).
Axes of the slice: x: 2, y: 2, z: 4, core: 2. Of those that a mesh axis runs over, the one named last changes fastest.
Arguments:
- source_v: float32 [2, 4, 2560, 768], P(None, 'col', 'row'), may hold values from -6 to 6
- source_omega: float32 [2, 4, 2560, 768], P(None, 'col', 'row'), may hold values from -6 to 6
- forward_map: float32 [768, 768], P('col'), may hold values from -0.21875 to 0.21875
- back_maps: float32 [2, 768, 768], P(None, 'col'), may hold values from -0.21875 to 0.21875
- eigenvalues: float32 [768], replicated, may hold values from 0.02 to 4
- penalty: float32 [768, 3840], P('row'), may hold values from 0.05 to 4
Outputs:
- v_field: float32 [2, 4, 2560, 768], P(None, 'col', 'row')
- omega_field: float32 [2, 4, 2560, 768], P(None, 'col', 'row')
The draws below stay inside these ranges and needn't reach their ends.
All inputs are finite; a program needn't handle non-finite values.
Results may differ from the reference program's by a relative error of at most 0.000098.
Values sent between devices are 32-bit elements; how exact they have to be, the bound alone decides.
A program may use at most 128 MiB of HBM per device.

```python
import math
import jax
import jax.numpy as jnp
from jax import lax

NY = 768
NZ = 3840
KX = 4
KZ = 2560


def block_levels(rng, extent, cuts, smallest, top_value):
    def one(position, blocks):
        heights = jax.random.uniform(jax.random.fold_in(jax.random.fold_in(rng, 6), position), (blocks,), jnp.float32, smallest / len(cuts), top_value / len(cuts))
        return jnp.repeat(jnp.exp(heights), extent[position] // blocks).reshape((-1,) + (1,) * (len(extent) - position - 1))

    loudness = one(*cuts[0])
    for cut in cuts[1:]:
        loudness = loudness * one(*cut)
    return loudness


def noise(own_key, extent, width, reach, split=(), kind=jnp.bfloat16):
    values = jax.random.normal(own_key, extent, jnp.float32) * width
    if len(split) > 0:
        values = block_levels(own_key, extent, split, -0.22, 0.18) * values
    return jnp.clip(values, min=-reach, max=reach).astype(kind)


def setup_inputs(seed: int = 0) -> dict:
    keys = jax.random.split(jax.random.key(seed), 7)
    return {
        "source_v": noise(keys[0], (2, KX, KZ, NY), 1.0, 6.0, ((1, 4), (2, 8)), jnp.float32),
        "source_omega": noise(keys[1], (2, KX, KZ, NY), 1.0, 6.0, ((1, 4), (2, 8)), jnp.float32),
        "forward_map": noise(keys[2], (NY, NY), NY ** -0.5, 0.21875, ((0, 4),), jnp.float32),
        "back_maps": noise(keys[3], (2, NY, NY), NY ** -0.5, 0.21875, ((1, 4),), jnp.float32),
        "eigenvalues": jnp.clip(jnp.exp(jax.random.uniform(keys[4], (NY,), jnp.float32, math.log(0.02), math.log(4.0))), 0.02, 4.0),
        "penalty": jnp.clip(jnp.exp(math.log(4.0) - 4.3820266 * jax.random.uniform(keys[5], (NY, NZ), jnp.float32) ** block_levels(keys[5], (NY, NZ), ((0, 8),), -0.2, 0.2)), 0.05, 4.0),
    }


def wave_numbers(count_modes, half_modes):
    index_all = jnp.arange(count_modes, dtype=jnp.int32)
    signed = jnp.where(index_all < half_modes, index_all, index_all - count_modes)
    return signed.astype(jnp.float32) * 8.0 / half_modes


def helm_scale(eigen_part, flow_wave, span_wave):
    return 1.0 / (1.0 + eigen_part + 0.05 * (flow_wave * flow_wave + span_wave * span_wave))


def form_velocity(flow_wave, span_wave, derivative, vorticity):
    wave_sq = jnp.maximum(flow_wave * flow_wave + span_wave * span_wave, 1.0)
    along_real = (span_wave * vorticity[1] - flow_wave * derivative[1]) / wave_sq
    along_imag = (flow_wave * derivative[0] - span_wave * vorticity[0]) / wave_sq
    across_real = -(span_wave * derivative[1] + flow_wave * vorticity[1]) / wave_sq
    across_imag = (span_wave * derivative[0] + flow_wave * vorticity[0]) / wave_sq
    return jnp.stack([along_real, along_imag]), jnp.stack([across_real, across_imag])


def form_vorticity(flow_wave, span_wave, along, across):
    real_part = flow_wave * across[1] - span_wave * along[1]
    imag_part = span_wave * along[0] - flow_wave * across[0]
    return jnp.stack([real_part, imag_part])


def reference(source_v, source_omega, forward_map, back_maps, eigenvalues, penalty):
    count_kz = source_v.shape[2]
    half_kz = count_kz // 2
    count_z = penalty.shape[1]
    count_y = source_v.shape[3]
    span_wave = wave_numbers(count_kz, half_kz)[:, None]
    flow_all = 0.5 * jnp.arange(source_v.shape[1], dtype=jnp.int32).astype(jnp.float32)
    factor_grid = jnp.transpose(1.0 / (1.0 + penalty))

    def one_mode(inputs):
        source_pair, flow_wave = inputs
        coeffs = jnp.einsum('fckn,jn->fckj', source_pair, forward_map, precision=lax.Precision.HIGHEST)
        coeffs = coeffs * helm_scale(eigenvalues[None, :], flow_wave, span_wave)
        values = jnp.einsum('yj,fckj->fcky', back_maps[0], coeffs, precision=lax.Precision.HIGHEST)
        derivative = jnp.einsum('yj,ckj->cky', back_maps[1], coeffs[0], precision=lax.Precision.HIGHEST)
        along, across = form_velocity(flow_wave, span_wave, derivative, values[1])
        velocity = jnp.stack([along, values[0], across])
        spectral = lax.complex(velocity[:, 0], velocity[:, 1])
        padding = jnp.zeros((3, count_z - count_kz, count_y), spectral.dtype)
        padded = jnp.concatenate([spectral[:, :half_kz], padding, spectral[:, half_kz:]], axis=1)
        physical = jnp.fft.ifft(padded, axis=1) * count_z
        physical = physical * factor_grid
        spectrum = jnp.fft.fft(physical, axis=1) / count_z
        kept = jnp.concatenate([spectrum[:, :half_kz], spectrum[:, count_z - half_kz:]], axis=1)
        result = jnp.stack([jnp.real(kept), jnp.imag(kept)], axis=1)
        vorticity = form_vorticity(flow_wave, span_wave, result[0], result[2])
        return jnp.stack([result[1], vorticity])

    sources = jnp.transpose(jnp.stack([source_v, source_omega]), (2, 0, 1, 3, 4))
    outputs = lax.map(one_mode, (sources, flow_all))
    v_field = jnp.transpose(outputs[:, 0], (1, 0, 2, 3))
    omega_field = jnp.transpose(outputs[:, 1], (1, 0, 2, 3))
    return v_field, omega_field
```

```python
import functools
import math

import jax
import jax.numpy as jnp
import ml_dtypes
import numpy as np
from jax import lax
from jax.experimental import pallas as pl
from jax.experimental.pallas import tpu as pltpu
from jax.sharding import PartitionSpec as P

HIGH = lax.Precision.HIGH
BLOCKS = 8
ROWS = 8


def helm_scale(eigen_part, flow_wave, span_wave):
    return 1.0 / (1.0 + eigen_part + 0.05 * (flow_wave * flow_wave + span_wave * span_wave))


def split_table(table):
    high = table.astype(ml_dtypes.bfloat16)
    low = (table - high.astype(np.float64)).astype(ml_dtypes.bfloat16)
    return high, low


@functools.lru_cache
def spanwise_tables(block, count_z):
    coarse = count_z // block
    order = [a0 + 3 * a1 for a0 in range(3) for a1 in range(4)]
    r = np.arange(block)[:, None]
    b = np.arange(block)[None, :]
    tables = []
    for a in order:
        angle = 2.0 * math.pi * ((r * (a + coarse * b)) % count_z) / count_z
        cos, sin = np.cos(angle), np.sin(angle)
        tables.append(np.block([[cos, sin], [-sin, cos]]))
    high, low = split_table(np.stack(tables))
    weights = np.zeros((3, 16), np.float32)
    for a0 in range(3):
        for s0 in range(4):
            first = 2.0 * math.pi * s0 * a0 / 12
            second = 2.0 * math.pi * (s0 + 8) * a0 / 12
            weights[a0, 4 * s0 : 4 * s0 + 4] = (
                math.cos(first),
                math.sin(first),
                math.cos(second),
                math.sin(second),
            )
    return high, low, weights


def split_value(value):
    high = value.astype(jnp.bfloat16)
    low = (value - high.astype(jnp.float32)).astype(jnp.bfloat16)
    return high, low


def spanwise_kernel(weight_ref, flow_ref, x_ref, kz_ref, fac_ref, high_ref, low_ref, out_ref, u_ref, y_ref):
    a0 = pl.program_id(0)
    a1 = pl.program_id(1)
    rows, width = x_ref.shape[1], x_ref.shape[2]
    block = width // 2
    local_y = rows // 3
    sign = jnp.where(lax.broadcasted_iota(jnp.int32, (ROWS, width), 1) < block, -1.0, 1.0)

    def times_i(value):
        return sign * pltpu.roll(value, block, 1)

    def coefficients(s0):
        return [weight_ref[a0, 4 * s0 + p] for p in range(4)]

    @pl.when(a1 == 0)
    def _():
        @pl.loop(0, rows // ROWS)
        def _(step):
            at = pl.ds(pl.multiple_of(step * ROWS, ROWS), ROWS)
            z = []
            for s0 in range(4):
                c1, s1, c2, s2 = coefficients(s0)
                first, second = x_ref[s0, at, :], x_ref[s0 + 4, at, :]
                z.append(c1 * first + c2 * second + times_i(s1 * first + s2 * second))
            even, odd = z[0] + z[2], z[0] - z[2]
            total, turned = z[1] + z[3], times_i(z[1] - z[3])
            u_ref[0, at, :] = even + total
            u_ref[1, at, :] = odd + turned
            u_ref[2, at, :] = even - total
            u_ref[3, at, :] = odd - turned

    dot = functools.partial(lax.dot_general, preferred_element_type=jnp.float32)
    plain = (((1,), (0,)), ((), ()))
    flipped = (((1,), (1,)), ((), ()))
    table_high, table_low = high_ref[0], low_ref[0]

    for field in range(3):
        at = pl.ds(field * local_y, local_y)
        high, low = split_value(u_ref[a1, at, :])
        physical = dot(high, table_high, plain) + dot(high, table_low, plain) + dot(low, table_high, plain)
        high, low = split_value(physical * fac_ref[0])
        u_ref[a1, at, :] = (
            dot(high, table_high, flipped) + dot(high, table_low, flipped) + dot(low, table_high, flipped)
        )

    @pl.when(a1 == 3)
    def _():
        @pl.when(a0 == 0)
        def _():
            y_ref[...] = jnp.zeros_like(y_ref)

        @pl.loop(0, rows // ROWS)
        def _(step):
            at = pl.ds(pl.multiple_of(step * ROWS, ROWS), ROWS)
            even, odd = u_ref[0, at, :] + u_ref[2, at, :], u_ref[0, at, :] - u_ref[2, at, :]
            total, turned = u_ref[1, at, :] + u_ref[3, at, :], times_i(u_ref[1, at, :] - u_ref[3, at, :])
            q = [even + total, odd - turned, even - total, odd + turned]
            for s0 in range(4):
                c1, s1, c2, s2 = coefficients(s0)
                rotated = times_i(q[s0])
                y_ref[s0, at, :] += c1 * q[s0] - s1 * rotated
                y_ref[s0 + 4, at, :] += c2 * q[s0] - s2 * rotated

        @pl.when(a0 == 2)
        def _():
            flow_wave = flow_ref[0]

            @pl.loop(0, local_y // ROWS)
            def _(step):
                def at(field):
                    return pl.ds(pl.multiple_of(field * local_y + step * ROWS, ROWS), ROWS)

                for s in range(BLOCKS):
                    mixed = kz_ref[s : s + 1, :] * y_ref[s, at(0), :] - flow_wave * y_ref[s, at(2), :]
                    out_ref[s, 0, at(0), :] = y_ref[s, at(1), :]
                    out_ref[s, 1, at(0), :] = times_i(mixed)


def spanwise_pass(data, kz_rows, flow_wave, factor, count_z):
    _, rows, width = data.shape
    local_y = rows // 3
    high, low, weights = spanwise_tables(width // 2, count_z)
    whole = pl.BlockSpec(memory_space=pltpu.VMEM)
    scalars = pl.BlockSpec(memory_space=pltpu.SMEM)
    flops = 2 * 2 * 3 * 12 * rows * width * width
    return pl.pallas_call(
        spanwise_kernel,
        grid=(3, 4),
        out_shape=jax.ShapeDtypeStruct((BLOCKS, 2, local_y, width), jnp.float32),
        in_specs=[
            scalars,
            scalars,
            whole,
            whole,
            pl.BlockSpec((1, local_y, width), lambda i, j: (4 * i + j, 0, 0)),
            pl.BlockSpec((1, width, width), lambda i, j: (4 * i + j, 0, 0)),
            pl.BlockSpec((1, width, width), lambda i, j: (4 * i + j, 0, 0)),
        ],
        out_specs=whole,
        scratch_shapes=[
            pltpu.VMEM((4, rows, width), jnp.float32),
            pltpu.VMEM((BLOCKS, rows, width), jnp.float32),
        ],
        compiler_params=pltpu.CompilerParams(vmem_limit_bytes=44 * 2**20),
        cost_estimate=pl.CostEstimate(flops=flops, bytes_accessed=4 * 12 * width * width, transcendentals=0),
        name="spanwise",
    )(jnp.asarray(weights), flow_wave.reshape(1), data, kz_rows, factor, jnp.asarray(high), jnp.asarray(low))


def gather_rows(block, axis):
    share = lax.axis_size("row")
    extent = block.shape[axis]
    if extent % (8 * share):
        return lax.all_gather(block, "col", axis=axis, tiled=True)
    piece = extent // share
    own = lax.dynamic_slice_in_dim(block, lax.axis_index("row") * piece, piece, axis)
    return lax.all_gather(own, ("col", "row"), axis=axis, tiled=True)


def shards(source_v, source_omega, forward_map, back_maps, eigenvalues, penalty):
    _, local_kx, local_kz, count_y = source_v.shape
    assert local_kx == 1
    share = lax.axis_size("row")
    count_kz = local_kz * share
    half_kz = count_kz // 2
    local_y, count_z = penalty.shape
    block = count_kz // BLOCKS
    coarse = count_z // block
    assert coarse == 12 and share % BLOCKS == 0
    flow_wave = 0.5 * lax.axis_index("col").astype(jnp.float32)

    def wave_of(index):
        return jnp.where(index < half_kz, index, index - count_kz).astype(jnp.float32) * 8.0 / half_kz

    span_local = wave_of(lax.axis_index("row") * local_kz + jnp.arange(local_kz, dtype=jnp.int32))
    span = jnp.concatenate([span_local, span_local])[None, :]
    sign = jnp.where(jnp.arange(2 * local_kz) < local_kz, 1.0, -1.0)[None, :]
    scaling = helm_scale(eigenvalues[:, None], flow_wave, span)
    wave_sq = jnp.maximum(flow_wave * flow_wave + span * span, 1.0)

    forward = gather_rows(forward_map, 0)
    back = gather_rows(back_maps, 1)

    def rows_of(source):
        return source.reshape(2 * local_kz, count_y)

    def turned_rows(source):
        return jnp.concatenate([source[1, 0], source[0, 0]], axis=0)

    def coefficients(rows):
        return jnp.einsum("jn,kn->jk", forward, rows, precision=HIGH) * scaling

    def back_of(which, coeffs):
        return jnp.einsum("yj,jk->yk", back[which], coeffs, precision=HIGH)

    value = back_of(0, coefficients(rows_of(source_v)))
    derivative = back_of(1, coefficients(turned_rows(source_v)))
    vorticity = back_of(0, coefficients(turned_rows(source_omega)))
    along = sign * (span * vorticity - flow_wave * derivative) / wave_sq
    across = -sign * (span * derivative + flow_wave * vorticity) / wave_sq

    def by_owner(field):
        return field.reshape(share, local_y, 2 * local_kz)

    fields = jnp.stack([by_owner(along), by_owner(value), by_owner(across)], axis=1)
    arrived = lax.all_to_all(fields, "row", split_axis=0, concat_axis=0)
    merge = share // BLOCKS
    data = arrived
    if merge > 1:
        data = arrived.reshape(BLOCKS, merge, 3 * local_y, 2, local_kz)
        data = jnp.transpose(data, (0, 2, 3, 1, 4))
    data = data.reshape(BLOCKS, 3 * local_y, 2 * block)

    kz_rows = wave_of(jnp.arange(count_kz, dtype=jnp.int32)).reshape(BLOCKS, block)
    kz_rows = jnp.concatenate([kz_rows, kz_rows], axis=1)
    factor = jnp.transpose(penalty.reshape(local_y, block, coarse), (2, 0, 1))
    factor = factor.reshape(4, 3, local_y, block).transpose(1, 0, 2, 3).reshape(coarse, local_y, block)
    factor = (1.0 / count_z) / (1.0 + factor)
    factor = jnp.concatenate([factor, factor], axis=2)
    result = spanwise_pass(data, kz_rows, flow_wave, factor, count_z)
    if merge > 1:
        result = result.reshape(BLOCKS, 2, local_y, 2, merge, local_kz)
        result = jnp.transpose(result, (0, 4, 1, 2, 3, 5))
    result = result.reshape(share, 2, local_y, 2 * local_kz)
    returned = lax.all_to_all(result, "row", split_axis=0, concat_axis=0)

    def placed(field):
        flat = returned[:, field].reshape(count_y, 2 * local_kz)
        return jnp.transpose(flat).reshape(2, 1, local_kz, count_y)

    return placed(0), placed(1)


def solution(mesh):
    placed = (
        P(None, "col", "row", None),
        P(None, "col", "row", None),
        P("col", None),
        P(None, "col", None),
        P(),
        P("row", None),
    )
    return jax.shard_map(
        shards,
        mesh=mesh,
        in_specs=placed,
        out_specs=(P(None, "col", "row", None), P(None, "col", "row", None)),
        check_vma=False,
    )
```

```python
import functools
import math

import jax
import jax.numpy as jnp
import ml_dtypes
import numpy as np
from jax import lax
from jax.experimental import pallas as pl
from jax.experimental.pallas import tpu as pltpu
from jax.sharding import PartitionSpec as P

HIGH = lax.Precision.HIGH
BLOCKS = 8
ROWS = 8


def helm_scale(eigen_part, flow_wave, span_wave):
    return 1.0 / (1.0 + eigen_part + 0.05 * (flow_wave * flow_wave + span_wave * span_wave))


def split_table(table):
    high = table.astype(ml_dtypes.bfloat16)
    low = (table - high.astype(np.float64)).astype(ml_dtypes.bfloat16)
    return high, low


@functools.lru_cache
def spanwise_tables(block, count_z):
    coarse = count_z // block
    order = [a0 + 3 * a1 for a0 in range(3) for a1 in range(4)]
    r = np.arange(block)[:, None]
    b = np.arange(block)[None, :]
    tables = []
    for a in order:
        angle = 2.0 * math.pi * ((r * (a + coarse * b)) % count_z) / count_z
        cos, sin = np.cos(angle), np.sin(angle)
        tables.append(np.block([[cos, sin], [-sin, cos]]))
    high, low = split_table(np.stack(tables))
    weights = np.zeros((3, 16), np.float32)
    for a0 in range(3):
        for s0 in range(4):
            first = 2.0 * math.pi * s0 * a0 / 12
            second = 2.0 * math.pi * (s0 + 8) * a0 / 12
            weights[a0, 4 * s0 : 4 * s0 + 4] = (
                math.cos(first),
                math.sin(first),
                math.cos(second),
                math.sin(second),
            )
    return high, low, weights


def split_value(value):
    high = value.astype(jnp.bfloat16)
    low = (value - high.astype(jnp.float32)).astype(jnp.bfloat16)
    return high, low


def spanwise_kernel(weight_ref, flow_ref, x_ref, kz_ref, fac_ref, high_ref, low_ref, out_ref, u_ref, y_ref):
    a0 = pl.program_id(0)
    a1 = pl.program_id(1)
    rows, width = x_ref.shape[1], x_ref.shape[2]
    block = width // 2
    local_y = rows // 3
    sign = jnp.where(lax.broadcasted_iota(jnp.int32, (ROWS, width), 1) < block, -1.0, 1.0)

    def times_i(value):
        return sign * pltpu.roll(value, block, 1)

    def coefficients(s0):
        return [weight_ref[a0, 4 * s0 + p] for p in range(4)]

    @pl.when(a1 == 0)
    def _():
        @pl.loop(0, rows // ROWS)
        def _(step):
            at = pl.ds(pl.multiple_of(step * ROWS, ROWS), ROWS)
            z = []
            for s0 in range(4):
                c1, s1, c2, s2 = coefficients(s0)
                first, second = x_ref[s0, at, :], x_ref[s0 + 4, at, :]
                z.append(c1 * first + c2 * second + times_i(s1 * first + s2 * second))
            even, odd = z[0] + z[2], z[0] - z[2]
            total, turned = z[1] + z[3], times_i(z[1] - z[3])
            u_ref[0, at, :] = even + total
            u_ref[1, at, :] = odd + turned
            u_ref[2, at, :] = even - total
            u_ref[3, at, :] = odd - turned

    dot = functools.partial(lax.dot_general, preferred_element_type=jnp.float32)
    plain = (((1,), (0,)), ((), ()))
    flipped = (((1,), (1,)), ((), ()))
    table_high, table_low = high_ref[0], low_ref[0]

    def product(value, dims):
        high, low = split_value(value)
        both = dot(jnp.concatenate([high, low], axis=0), table_high, dims)
        return both[:rows] + both[rows:] + dot(high, table_low, dims)

    physical = product(u_ref[a1], plain).reshape(3, local_y, width)
    u_ref[a1] = product((physical * fac_ref[0][None]).reshape(rows, width), flipped)

    @pl.when(a1 == 3)
    def _():
        @pl.when(a0 == 0)
        def _():
            y_ref[...] = jnp.zeros_like(y_ref)

        @pl.loop(0, rows // ROWS)
        def _(step):
            at = pl.ds(pl.multiple_of(step * ROWS, ROWS), ROWS)
            even, odd = u_ref[0, at, :] + u_ref[2, at, :], u_ref[0, at, :] - u_ref[2, at, :]
            total, turned = u_ref[1, at, :] + u_ref[3, at, :], times_i(u_ref[1, at, :] - u_ref[3, at, :])
            q = [even + total, odd - turned, even - total, odd + turned]
            for s0 in range(4):
                c1, s1, c2, s2 = coefficients(s0)
                rotated = times_i(q[s0])
                y_ref[s0, at, :] += c1 * q[s0] - s1 * rotated
                y_ref[s0 + 4, at, :] += c2 * q[s0] - s2 * rotated

        @pl.when(a0 == 2)
        def _():
            flow_wave = flow_ref[0]

            @pl.loop(0, local_y // ROWS)
            def _(step):
                def at(field):
                    return pl.ds(pl.multiple_of(field * local_y + step * ROWS, ROWS), ROWS)

                for s in range(BLOCKS):
                    mixed = kz_ref[s : s + 1, :] * y_ref[s, at(0), :] - flow_wave * y_ref[s, at(2), :]
                    out_ref[s, 0, at(0), :] = y_ref[s, at(1), :]
                    out_ref[s, 1, at(0), :] = times_i(mixed)


def spanwise_pass(data, kz_rows, flow_wave, factor, count_z):
    _, rows, width = data.shape
    local_y = rows // 3
    high, low, weights = spanwise_tables(width // 2, count_z)
    whole = pl.BlockSpec(memory_space=pltpu.VMEM)
    scalars = pl.BlockSpec(memory_space=pltpu.SMEM)
    flops = 2 * 2 * 3 * 12 * rows * width * width
    return pl.pallas_call(
        spanwise_kernel,
        grid=(3, 4),
        out_shape=jax.ShapeDtypeStruct((BLOCKS, 2, local_y, width), jnp.float32),
        in_specs=[
            scalars,
            scalars,
            whole,
            whole,
            pl.BlockSpec((1, local_y, width), lambda i, j: (4 * i + j, 0, 0)),
            pl.BlockSpec((1, width, width), lambda i, j: (4 * i + j, 0, 0)),
            pl.BlockSpec((1, width, width), lambda i, j: (4 * i + j, 0, 0)),
        ],
        out_specs=whole,
        scratch_shapes=[
            pltpu.VMEM((4, rows, width), jnp.float32),
            pltpu.VMEM((BLOCKS, rows, width), jnp.float32),
        ],
        compiler_params=pltpu.CompilerParams(vmem_limit_bytes=44 * 2**20),
        cost_estimate=pl.CostEstimate(flops=flops, bytes_accessed=4 * 12 * width * width, transcendentals=0),
        name="spanwise",
    )(jnp.asarray(weights), flow_wave.reshape(1), data, kz_rows, factor, jnp.asarray(high), jnp.asarray(low))


def gather_rows(block, axis):
    share = lax.axis_size("row")
    extent = block.shape[axis]
    if extent % (8 * share):
        return lax.all_gather(block, "col", axis=axis, tiled=True)
    piece = extent // share
    own = lax.dynamic_slice_in_dim(block, lax.axis_index("row") * piece, piece, axis)
    column = lax.all_gather(own, "col", axis=axis, tiled=False)
    everyone = lax.all_gather(column, "row", axis=axis + 1, tiled=False)
    shape = block.shape[:axis] + (extent * lax.axis_size("col"),) + block.shape[axis + 1 :]
    return everyone.reshape(shape)


def shards(source_v, source_omega, forward_map, back_maps, eigenvalues, penalty):
    _, local_kx, local_kz, count_y = source_v.shape
    assert local_kx == 1
    share = lax.axis_size("row")
    count_kz = local_kz * share
    half_kz = count_kz // 2
    local_y, count_z = penalty.shape
    block = count_kz // BLOCKS
    coarse = count_z // block
    assert coarse == 12 and share % BLOCKS == 0
    flow_wave = 0.5 * lax.axis_index("col").astype(jnp.float32)

    def wave_of(index):
        return jnp.where(index < half_kz, index, index - count_kz).astype(jnp.float32) * 8.0 / half_kz

    span_local = wave_of(lax.axis_index("row") * local_kz + jnp.arange(local_kz, dtype=jnp.int32))
    span = jnp.concatenate([span_local, span_local])[None, :]
    sign = jnp.where(jnp.arange(2 * local_kz) < local_kz, 1.0, -1.0)[None, :]
    scaling = helm_scale(eigenvalues[:, None], flow_wave, span)
    wave_sq = jnp.maximum(flow_wave * flow_wave + span * span, 1.0)

    forward = gather_rows(forward_map, 0)
    back = gather_rows(back_maps, 1)

    def rows_of(source):
        return source.reshape(2 * local_kz, count_y)

    def turned_rows(source):
        return jnp.concatenate([source[1, 0], source[0, 0]], axis=0)

    def coefficients(rows):
        return jnp.einsum("jn,kn->jk", forward, rows, precision=HIGH) * scaling

    def back_of(which, coeffs):
        return jnp.einsum("yj,jk->yk", back[which], coeffs, precision=HIGH)

    value = back_of(0, coefficients(rows_of(source_v)))
    derivative = back_of(1, coefficients(turned_rows(source_v)))
    vorticity = back_of(0, coefficients(turned_rows(source_omega)))
    along = sign * (span * vorticity - flow_wave * derivative) / wave_sq
    across = -sign * (span * derivative + flow_wave * vorticity) / wave_sq

    def by_owner(field):
        return field.reshape(share, local_y, 2 * local_kz)

    fields = jnp.stack([by_owner(along), by_owner(value), by_owner(across)], axis=1)
    arrived = lax.all_to_all(fields, "row", split_axis=0, concat_axis=0)
    merge = share // BLOCKS
    data = arrived
    if merge > 1:
        data = arrived.reshape(BLOCKS, merge, 3 * local_y, 2, local_kz)
        data = jnp.transpose(data, (0, 2, 3, 1, 4))
    data = data.reshape(BLOCKS, 3 * local_y, 2 * block)

    kz_rows = wave_of(jnp.arange(count_kz, dtype=jnp.int32)).reshape(BLOCKS, block)
    kz_rows = jnp.concatenate([kz_rows, kz_rows], axis=1)
    factor = jnp.transpose(penalty.reshape(local_y, block, coarse), (2, 0, 1))
    factor = factor.reshape(4, 3, local_y, block).transpose(1, 0, 2, 3).reshape(coarse, local_y, block)
    factor = (1.0 / count_z) / (1.0 + factor)
    factor = jnp.concatenate([factor, factor], axis=2)
    result = spanwise_pass(data, kz_rows, flow_wave, factor, count_z)
    if merge > 1:
        result = result.reshape(BLOCKS, 2, local_y, 2, merge, local_kz)
        result = jnp.transpose(result, (0, 4, 1, 2, 3, 5))
    result = result.reshape(share, 2, local_y, 2 * local_kz)
    returned = lax.all_to_all(result, "row", split_axis=0, concat_axis=0)

    def placed(field):
        flat = returned[:, field].reshape(count_y, 2 * local_kz)
        return jnp.transpose(flat).reshape(2, 1, local_kz, count_y)

    return placed(0), placed(1)


def solution(mesh):
    placed = (
        P(None, "col", "row", None),
        P(None, "col", "row", None),
        P("col", None),
        P(None, "col", None),
        P(),
        P("row", None),
    )
    return jax.shard_map(
        shards,
        mesh=mesh,
        in_specs=placed,
        out_specs=(P(None, "col", "row", None), P(None, "col", "row", None)),
        check_vma=False,
    )
```

```python
import functools
import math

import jax
import jax.numpy as jnp
import ml_dtypes
import numpy as np
from jax import lax
from jax.experimental import pallas as pl
from jax.experimental.pallas import tpu as pltpu
from jax.sharding import PartitionSpec as P

HIGH = lax.Precision.HIGH
BLOCKS = 8
ROWS = 8


def helm_scale(eigen_part, flow_wave, span_wave):
    return 1.0 / (1.0 + eigen_part + 0.05 * (flow_wave * flow_wave + span_wave * span_wave))


def split_table(table):
    high = table.astype(ml_dtypes.bfloat16)
    low = (table - high.astype(np.float64)).astype(ml_dtypes.bfloat16)
    return high, low


@functools.lru_cache
def spanwise_tables(block, count_z):
    coarse = count_z // block
    order = [a0 + 3 * a1 for a0 in range(3) for a1 in range(4)]
    r = np.arange(block)[:, None]
    b = np.arange(block)[None, :]
    tables = []
    for a in order:
        angle = 2.0 * math.pi * ((r * (a + coarse * b)) % count_z) / count_z
        cos, sin = np.cos(angle), np.sin(angle)
        tables.append(np.block([[cos, sin], [-sin, cos]]))
    high, low = split_table(np.stack(tables))
    weights = np.zeros((3, 16), np.float32)
    for a0 in range(3):
        for s0 in range(4):
            first = 2.0 * math.pi * s0 * a0 / 12
            second = 2.0 * math.pi * (s0 + 8) * a0 / 12
            weights[a0, 4 * s0 : 4 * s0 + 4] = (
                math.cos(first),
                math.sin(first),
                math.cos(second),
                math.sin(second),
            )
    return high, low, weights


def split_value(value):
    high = value.astype(jnp.bfloat16)
    low = (value - high.astype(jnp.float32)).astype(jnp.bfloat16)
    return high, low


def spanwise_kernel(weight_ref, flow_ref, x_ref, kz_ref, fac_ref, high_ref, low_ref, out_ref, u_ref, y_ref):
    a0 = pl.program_id(0)
    a1 = pl.program_id(1)
    rows, width = x_ref.shape[1], x_ref.shape[2]
    block = width // 2
    local_y = rows // 3
    sign = jnp.where(lax.broadcasted_iota(jnp.int32, (ROWS, width), 1) < block, -1.0, 1.0)

    def times_i(value):
        return sign * pltpu.roll(value, block, 1)

    def coefficients(s0):
        return [weight_ref[a0, 4 * s0 + p] for p in range(4)]

    @pl.when(a1 == 0)
    def _():
        @pl.loop(0, rows // ROWS, unroll=3)
        def _(step):
            at = pl.ds(pl.multiple_of(step * ROWS, ROWS), ROWS)
            z = []
            for s0 in range(4):
                c1, s1, c2, s2 = coefficients(s0)
                first, second = x_ref[s0, at, :], x_ref[s0 + 4, at, :]
                z.append(c1 * first + c2 * second + times_i(s1 * first + s2 * second))
            even, odd = z[0] + z[2], z[0] - z[2]
            total, turned = z[1] + z[3], times_i(z[1] - z[3])
            u_ref[0, at, :] = even + total
            u_ref[1, at, :] = odd + turned
            u_ref[2, at, :] = even - total
            u_ref[3, at, :] = odd - turned

    dot = functools.partial(lax.dot_general, preferred_element_type=jnp.float32)
    plain = (((1,), (0,)), ((), ()))
    flipped = (((1,), (1,)), ((), ()))
    table_high, table_low = high_ref[0], low_ref[0]

    def product(value, dims):
        high, low = split_value(value)
        both = dot(jnp.concatenate([high, low], axis=0), table_high, dims)
        return both[:rows] + both[rows:] + dot(high, table_low, dims)

    physical = product(u_ref[a1], plain).reshape(3, local_y, width)
    u_ref[a1] = product((physical * fac_ref[0][None]).reshape(rows, width), flipped)

    @pl.when(a1 == 3)
    def _():
        @pl.when(a0 == 0)
        def _():
            y_ref[...] = jnp.zeros_like(y_ref)

        @pl.loop(0, rows // ROWS, unroll=3)
        def _(step):
            at = pl.ds(pl.multiple_of(step * ROWS, ROWS), ROWS)
            even, odd = u_ref[0, at, :] + u_ref[2, at, :], u_ref[0, at, :] - u_ref[2, at, :]
            total, turned = u_ref[1, at, :] + u_ref[3, at, :], times_i(u_ref[1, at, :] - u_ref[3, at, :])
            q = [even + total, odd - turned, even - total, odd + turned]
            for s0 in range(4):
                c1, s1, c2, s2 = coefficients(s0)
                rotated = times_i(q[s0])
                y_ref[s0, at, :] += c1 * q[s0] - s1 * rotated
                y_ref[s0 + 4, at, :] += c2 * q[s0] - s2 * rotated

        @pl.when(a0 == 2)
        def _():
            flow_wave = flow_ref[0]

            @pl.loop(0, local_y // ROWS)
            def _(step):
                def at(field):
                    return pl.ds(pl.multiple_of(field * local_y + step * ROWS, ROWS), ROWS)

                for s in range(BLOCKS):
                    mixed = kz_ref[s : s + 1, :] * y_ref[s, at(0), :] - flow_wave * y_ref[s, at(2), :]
                    out_ref[s, 0, at(0), :] = y_ref[s, at(1), :]
                    out_ref[s, 1, at(0), :] = times_i(mixed)


def spanwise_pass(data, kz_rows, flow_wave, factor, count_z):
    _, rows, width = data.shape
    local_y = rows // 3
    high, low, weights = spanwise_tables(width // 2, count_z)
    whole = pl.BlockSpec(memory_space=pltpu.VMEM)
    scalars = pl.BlockSpec(memory_space=pltpu.SMEM)
    flops = 2 * 2 * 3 * 12 * rows * width * width
    return pl.pallas_call(
        spanwise_kernel,
        grid=(3, 4),
        out_shape=jax.ShapeDtypeStruct((BLOCKS, 2, local_y, width), jnp.float32),
        in_specs=[
            scalars,
            scalars,
            whole,
            whole,
            pl.BlockSpec((1, local_y, width), lambda i, j: (4 * i + j, 0, 0)),
            pl.BlockSpec((1, width, width), lambda i, j: (4 * i + j, 0, 0)),
            pl.BlockSpec((1, width, width), lambda i, j: (4 * i + j, 0, 0)),
        ],
        out_specs=whole,
        scratch_shapes=[
            pltpu.VMEM((4, rows, width), jnp.float32),
            pltpu.VMEM((BLOCKS, rows, width), jnp.float32),
        ],
        compiler_params=pltpu.CompilerParams(vmem_limit_bytes=44 * 2**20),
        cost_estimate=pl.CostEstimate(flops=flops, bytes_accessed=4 * 12 * width * width, transcendentals=0),
        name="spanwise",
    )(jnp.asarray(weights), flow_wave.reshape(1), data, kz_rows, factor, jnp.asarray(high), jnp.asarray(low))


def gather_maps(forward_map, back_maps):
    share = lax.axis_size("row")
    extent, count_y = forward_map.shape
    if extent % (8 * share):
        forward = lax.all_gather(forward_map, "col", axis=0, tiled=True)
        return forward, lax.all_gather(back_maps, "col", axis=1, tiled=True)
    piece = extent // share
    start = lax.axis_index("row") * piece
    own = [lax.dynamic_slice_in_dim(forward_map, start, piece, 0)[None]]
    own.append(lax.dynamic_slice_in_dim(back_maps, start, piece, 1))
    columns = lax.all_gather(jnp.concatenate(own, axis=0), "col", axis=1, tiled=False)

    def everyone(part):
        rows = lax.all_gather(part, "row", axis=2, tiled=False)
        return rows.reshape(part.shape[0], extent * lax.axis_size("col"), count_y)

    return everyone(columns[:1])[0], everyone(columns[1:])


def shards(source_v, source_omega, forward_map, back_maps, eigenvalues, penalty):
    _, local_kx, local_kz, count_y = source_v.shape
    assert local_kx == 1
    share = lax.axis_size("row")
    count_kz = local_kz * share
    half_kz = count_kz // 2
    local_y, count_z = penalty.shape
    block = count_kz // BLOCKS
    coarse = count_z // block
    assert coarse == 12 and share % BLOCKS == 0
    flow_wave = 0.5 * lax.axis_index("col").astype(jnp.float32)

    def wave_of(index):
        return jnp.where(index < half_kz, index, index - count_kz).astype(jnp.float32) * 8.0 / half_kz

    span_local = wave_of(lax.axis_index("row") * local_kz + jnp.arange(local_kz, dtype=jnp.int32))
    span = jnp.concatenate([span_local, span_local])[None, :]
    sign = jnp.where(jnp.arange(2 * local_kz) < local_kz, 1.0, -1.0)[None, :]
    scaling = helm_scale(eigenvalues[:, None], flow_wave, span)
    wave_sq = jnp.maximum(flow_wave * flow_wave + span * span, 1.0)

    forward, back = gather_maps(forward_map, back_maps)

    def rows_of(source):
        return source.reshape(2 * local_kz, count_y)

    def turned_rows(source):
        return jnp.concatenate([source[1, 0], source[0, 0]], axis=0)

    def coefficients(rows):
        return jnp.einsum("jn,kn->jk", forward, rows, precision=HIGH) * scaling

    def back_of(which, coeffs):
        return jnp.einsum("yj,jk->yk", back[which], coeffs, precision=HIGH)

    value = back_of(0, coefficients(rows_of(source_v)))
    derivative = back_of(1, coefficients(turned_rows(source_v)))
    vorticity = back_of(0, coefficients(turned_rows(source_omega)))
    along = sign * (span * vorticity - flow_wave * derivative) / wave_sq
    across = -sign * (span * derivative + flow_wave * vorticity) / wave_sq

    def by_owner(field):
        return field.reshape(share, local_y, 2 * local_kz)

    fields = jnp.stack([by_owner(along), by_owner(value), by_owner(across)], axis=1)
    arrived = lax.all_to_all(fields, "row", split_axis=0, concat_axis=0)
    merge = share // BLOCKS
    data = arrived
    if merge > 1:
        data = arrived.reshape(BLOCKS, merge, 3 * local_y, 2, local_kz)
        data = jnp.transpose(data, (0, 2, 3, 1, 4))
    data = data.reshape(BLOCKS, 3 * local_y, 2 * block)

    kz_rows = wave_of(jnp.arange(count_kz, dtype=jnp.int32)).reshape(BLOCKS, block)
    kz_rows = jnp.concatenate([kz_rows, kz_rows], axis=1)
    factor = jnp.transpose(penalty.reshape(local_y, block, coarse), (2, 0, 1))
    factor = factor.reshape(4, 3, local_y, block).transpose(1, 0, 2, 3).reshape(coarse, local_y, block)
    factor = (1.0 / count_z) / (1.0 + factor)
    factor = jnp.concatenate([factor, factor], axis=2)
    result = spanwise_pass(data, kz_rows, flow_wave, factor, count_z)
    if merge > 1:
        result = result.reshape(BLOCKS, 2, local_y, 2, merge, local_kz)
        result = jnp.transpose(result, (0, 4, 1, 2, 3, 5))
    result = result.reshape(share, 2, local_y, 2 * local_kz)
    returned = lax.all_to_all(result, "row", split_axis=0, concat_axis=0)

    def placed(field):
        flat = returned[:, field].reshape(count_y, 2 * local_kz)
        return jnp.transpose(flat).reshape(2, 1, local_kz, count_y)

    return placed(0), placed(1)


def solution(mesh):
    placed = (
        P(None, "col", "row", None),
        P(None, "col", "row", None),
        P("col", None),
        P(None, "col", None),
        P(),
        P("row", None),
    )
    return jax.shard_map(
        shards,
        mesh=mesh,
        in_specs=placed,
        out_specs=(P(None, "col", "row", None), P(None, "col", "row", None)),
        check_vma=False,
    )
```

```python
import functools
import math

import jax
import jax.numpy as jnp
import ml_dtypes
import numpy as np
from jax import lax
from jax.experimental import pallas as pl
from jax.experimental.pallas import tpu as pltpu
from jax.sharding import PartitionSpec as P

HIGH = lax.Precision.HIGH
BLOCKS = 8
ROWS = 8


def helm_scale(eigen_part, flow_wave, span_wave):
    return 1.0 / (1.0 + eigen_part + 0.05 * (flow_wave * flow_wave + span_wave * span_wave))


def split_table(table):
    high = table.astype(ml_dtypes.bfloat16)
    low = (table - high.astype(np.float64)).astype(ml_dtypes.bfloat16)
    return high, low


@functools.lru_cache
def spanwise_tables(block, count_z):
    coarse = count_z // block
    order = [a0 + 3 * a1 for a0 in range(3) for a1 in range(4)]
    r = np.arange(block)[:, None]
    b = np.arange(block)[None, :]
    tables = []
    for a in order:
        angle = 2.0 * math.pi * ((r * (a + coarse * b)) % count_z) / count_z
        cos, sin = np.cos(angle), np.sin(angle)
        tables.append(np.block([[cos, sin], [-sin, cos]]))
    high, low = split_table(np.stack(tables))
    weights = np.zeros((3, 16), np.float32)
    for a0 in range(3):
        for s0 in range(4):
            first = 2.0 * math.pi * s0 * a0 / 12
            second = 2.0 * math.pi * (s0 + 8) * a0 / 12
            weights[a0, 4 * s0 : 4 * s0 + 4] = (
                math.cos(first),
                math.sin(first),
                math.cos(second),
                math.sin(second),
            )
    return high, low, weights


def split_value(value):
    high = value.astype(jnp.bfloat16)
    low = (value - high.astype(jnp.float32)).astype(jnp.bfloat16)
    return high, low


def spanwise_kernel(weight_ref, flow_ref, x_ref, kz_ref, fac_ref, high_ref, low_ref, out_ref, u_ref, y_ref):
    a0 = pl.program_id(0)
    a1 = pl.program_id(1)
    rows, width = x_ref.shape[1], x_ref.shape[2]
    block = width // 2
    fields = x_ref.shape[1] // fac_ref.shape[1]
    local_y = rows // fields
    sign = jnp.where(lax.broadcasted_iota(jnp.int32, (ROWS, width), 1) < block, -1.0, 1.0)

    def times_i(value):
        return sign * pltpu.roll(value, block, 1)

    def coefficients(s0):
        return [weight_ref[a0, 4 * s0 + p] for p in range(4)]

    @pl.when(a1 == 0)
    def _():
        @pl.loop(0, rows // ROWS, unroll=3)
        def _(step):
            at = pl.ds(pl.multiple_of(step * ROWS, ROWS), ROWS)
            z = []
            for s0 in range(4):
                c1, s1, c2, s2 = coefficients(s0)
                first, second = x_ref[s0, at, :], x_ref[s0 + 4, at, :]
                z.append(c1 * first + c2 * second + times_i(s1 * first + s2 * second))
            even, odd = z[0] + z[2], z[0] - z[2]
            total, turned = z[1] + z[3], times_i(z[1] - z[3])
            u_ref[0, at, :] = even + total
            u_ref[1, at, :] = odd + turned
            u_ref[2, at, :] = even - total
            u_ref[3, at, :] = odd - turned

    dot = functools.partial(lax.dot_general, preferred_element_type=jnp.float32)
    plain = (((1,), (0,)), ((), ()))
    flipped = (((1,), (1,)), ((), ()))
    table_high, table_low = high_ref[0], low_ref[0]

    def product(value, dims):
        high, low = split_value(value)
        both = dot(jnp.concatenate([high, low], axis=0), table_high, dims)
        return both[:rows] + both[rows:] + dot(high, table_low, dims)

    physical = product(u_ref[a1], plain).reshape(fields, local_y, width)
    u_ref[a1] = product((physical * fac_ref[0][None]).reshape(rows, width), flipped)

    @pl.when(a1 == 3)
    def _():
        @pl.when(a0 == 0)
        def _():
            y_ref[...] = jnp.zeros_like(y_ref)

        @pl.loop(0, rows // ROWS, unroll=3)
        def _(step):
            at = pl.ds(pl.multiple_of(step * ROWS, ROWS), ROWS)
            even, odd = u_ref[0, at, :] + u_ref[2, at, :], u_ref[0, at, :] - u_ref[2, at, :]
            total, turned = u_ref[1, at, :] + u_ref[3, at, :], times_i(u_ref[1, at, :] - u_ref[3, at, :])
            q = [even + total, odd - turned, even - total, odd + turned]
            for s0 in range(4):
                c1, s1, c2, s2 = coefficients(s0)
                rotated = times_i(q[s0])
                y_ref[s0, at, :] += c1 * q[s0] - s1 * rotated
                y_ref[s0 + 4, at, :] += c2 * q[s0] - s2 * rotated

        @pl.when(a0 == 2)
        def _():
            flow_wave = flow_ref[0]

            @pl.loop(0, local_y // ROWS)
            def _(step):
                def at(field):
                    return pl.ds(pl.multiple_of(field * local_y + step * ROWS, ROWS), ROWS)

                for s in range(BLOCKS):
                    if fields == 1:
                        out_ref[s, at(0), :] = y_ref[s, at(0), :]
                    else:
                        mixed = kz_ref[s : s + 1, :] * y_ref[s, at(0), :] - flow_wave * y_ref[s, at(1), :]
                        out_ref[s, at(0), :] = times_i(mixed)


def spanwise_pass(data, kz_rows, flow_wave, factor, count_z):
    _, rows, width = data.shape
    local_y = factor.shape[1]
    high, low, weights = spanwise_tables(width // 2, count_z)
    whole = pl.BlockSpec(memory_space=pltpu.VMEM)
    scalars = pl.BlockSpec(memory_space=pltpu.SMEM)
    flops = 2 * 2 * 3 * 12 * rows * width * width
    return pl.pallas_call(
        spanwise_kernel,
        grid=(3, 4),
        out_shape=jax.ShapeDtypeStruct((BLOCKS, local_y, width), jnp.float32),
        in_specs=[
            scalars,
            scalars,
            whole,
            whole,
            pl.BlockSpec((1, local_y, width), lambda i, j: (4 * i + j, 0, 0)),
            pl.BlockSpec((1, width, width), lambda i, j: (4 * i + j, 0, 0)),
            pl.BlockSpec((1, width, width), lambda i, j: (4 * i + j, 0, 0)),
        ],
        out_specs=whole,
        scratch_shapes=[
            pltpu.VMEM((4, rows, width), jnp.float32),
            pltpu.VMEM((BLOCKS, rows, width), jnp.float32),
        ],
        compiler_params=pltpu.CompilerParams(vmem_limit_bytes=44 * 2**20),
        cost_estimate=pl.CostEstimate(flops=flops, bytes_accessed=4 * 12 * width * width, transcendentals=0),
        name="spanwise_v" if rows == local_y else "spanwise_omega",
    )(jnp.asarray(weights), flow_wave.reshape(1), data, kz_rows, factor, jnp.asarray(high), jnp.asarray(low))


def gather_maps(forward_map, back_maps):
    share = lax.axis_size("row")
    extent, count_y = forward_map.shape
    if extent % (8 * share):
        forward = lax.all_gather(forward_map, "col", axis=0, tiled=True)
        return forward, lax.all_gather(back_maps, "col", axis=1, tiled=True)
    piece = extent // share
    start = lax.axis_index("row") * piece
    own = [lax.dynamic_slice_in_dim(forward_map, start, piece, 0)[None]]
    own.append(lax.dynamic_slice_in_dim(back_maps, start, piece, 1))
    columns = lax.all_gather(jnp.concatenate(own, axis=0), "col", axis=1, tiled=False)

    def everyone(part):
        rows = lax.all_gather(part, "row", axis=2, tiled=False)
        return rows.reshape(part.shape[0], extent * lax.axis_size("col"), count_y)

    return everyone(columns[:1])[0], everyone(columns[1:])


def shards(source_v, source_omega, forward_map, back_maps, eigenvalues, penalty):
    _, local_kx, local_kz, count_y = source_v.shape
    assert local_kx == 1
    share = lax.axis_size("row")
    count_kz = local_kz * share
    half_kz = count_kz // 2
    local_y, count_z = penalty.shape
    block = count_kz // BLOCKS
    coarse = count_z // block
    assert coarse == 12 and share % BLOCKS == 0
    flow_wave = 0.5 * lax.axis_index("col").astype(jnp.float32)

    def wave_of(index):
        return jnp.where(index < half_kz, index, index - count_kz).astype(jnp.float32) * 8.0 / half_kz

    span_local = wave_of(lax.axis_index("row") * local_kz + jnp.arange(local_kz, dtype=jnp.int32))
    span = jnp.concatenate([span_local, span_local])[None, :]
    sign = jnp.where(jnp.arange(2 * local_kz) < local_kz, 1.0, -1.0)[None, :]
    scaling = helm_scale(eigenvalues[:, None], flow_wave, span)
    wave_sq = jnp.maximum(flow_wave * flow_wave + span * span, 1.0)

    forward, back = gather_maps(forward_map, back_maps)

    def rows_of(source):
        return source.reshape(2 * local_kz, count_y)

    def turned_rows(source):
        return jnp.concatenate([source[1, 0], source[0, 0]], axis=0)

    def coefficients(rows):
        return jnp.einsum("jn,kn->jk", forward, rows, precision=HIGH) * scaling

    def back_of(which, coeffs):
        return jnp.einsum("yj,jk->yk", back[which], coeffs, precision=HIGH)

    value = back_of(0, coefficients(rows_of(source_v)))
    derivative = back_of(1, coefficients(turned_rows(source_v)))
    vorticity = back_of(0, coefficients(turned_rows(source_omega)))
    along = sign * (span * vorticity - flow_wave * derivative) / wave_sq
    across = -sign * (span * derivative + flow_wave * vorticity) / wave_sq

    def by_owner(field):
        return field.reshape(share, local_y, 2 * local_kz)

    merge = share // BLOCKS

    def sent(*parts):
        fields = jnp.stack([by_owner(part) for part in parts], axis=1)
        data = lax.all_to_all(fields, "row", split_axis=0, concat_axis=0)
        rows = len(parts) * local_y
        if merge > 1:
            data = data.reshape(BLOCKS, merge, rows, 2, local_kz)
            data = jnp.transpose(data, (0, 2, 3, 1, 4))
        return data.reshape(BLOCKS, rows, 2 * block)

    data_v = sent(value)
    data_omega = sent(along, across)

    kz_rows = wave_of(jnp.arange(count_kz, dtype=jnp.int32)).reshape(BLOCKS, block)
    kz_rows = jnp.concatenate([kz_rows, kz_rows], axis=1)
    factor = jnp.transpose(penalty.reshape(local_y, block, coarse), (2, 0, 1))
    factor = factor.reshape(4, 3, local_y, block).transpose(1, 0, 2, 3).reshape(coarse, local_y, block)
    factor = (1.0 / count_z) / (1.0 + factor)
    factor = jnp.concatenate([factor, factor], axis=2)

    def finished(data):
        result = spanwise_pass(data, kz_rows, flow_wave, factor, count_z)
        if merge > 1:
            result = result.reshape(BLOCKS, local_y, 2, merge, local_kz)
            result = jnp.transpose(result, (0, 3, 1, 2, 4))
        result = result.reshape(share, local_y, 2 * local_kz)
        returned = lax.all_to_all(result, "row", split_axis=0, concat_axis=0)
        flat = returned.reshape(count_y, 2 * local_kz)
        return jnp.transpose(flat).reshape(2, 1, local_kz, count_y)

    return finished(data_v), finished(data_omega)


def solution(mesh):
    placed = (
        P(None, "col", "row", None),
        P(None, "col", "row", None),
        P("col", None),
        P(None, "col", None),
        P(),
        P("row", None),
    )
    return jax.shard_map(
        shards,
        mesh=mesh,
        in_specs=placed,
        out_specs=(P(None, "col", "row", None), P(None, "col", "row", None)),
        check_vma=False,
    )
```

```python
import functools
import math

import jax
import jax.numpy as jnp
import ml_dtypes
import numpy as np
from jax import lax
from jax.experimental import pallas as pl
from jax.experimental.pallas import tpu as pltpu
from jax.sharding import PartitionSpec as P

HIGH = lax.Precision.HIGH
BLOCKS = 8
ROWS = 8


def helm_scale(eigen_part, flow_wave, span_wave):
    return 1.0 / (1.0 + eigen_part + 0.05 * (flow_wave * flow_wave + span_wave * span_wave))


def split_table(table):
    high = table.astype(ml_dtypes.bfloat16)
    low = (table - high.astype(np.float64)).astype(ml_dtypes.bfloat16)
    return high, low


@functools.lru_cache
def spanwise_tables(block, count_z):
    coarse = count_z // block
    order = [a0 + 3 * a1 for a0 in range(3) for a1 in range(4)]
    r = np.arange(block)[:, None]
    b = np.arange(block)[None, :]
    tables = []
    for a in order:
        angle = 2.0 * math.pi * ((r * (a + coarse * b)) % count_z) / count_z
        cos, sin = np.cos(angle), np.sin(angle)
        tables.append(np.block([[cos, sin], [-sin, cos]]))
    high, low = split_table(np.stack(tables))
    weights = np.zeros((3, 16), np.float32)
    for a0 in range(3):
        for s0 in range(4):
            first = 2.0 * math.pi * s0 * a0 / 12
            second = 2.0 * math.pi * (s0 + 8) * a0 / 12
            weights[a0, 4 * s0 : 4 * s0 + 4] = (
                math.cos(first),
                math.sin(first),
                math.cos(second),
                math.sin(second),
            )
    return high, low, weights


def split_value(value):
    high = value.astype(jnp.bfloat16)
    low = (value - high.astype(jnp.float32)).astype(jnp.bfloat16)
    return high, low


def spanwise_kernel(weight_ref, flow_ref, x_ref, kz_ref, fac_ref, high_ref, low_ref, out_ref, u_ref, y_ref):
    a0 = pl.program_id(0)
    a1 = pl.program_id(1)
    rows, width = x_ref.shape[1], x_ref.shape[2]
    block = width // 2
    fields = x_ref.shape[1] // fac_ref.shape[1]
    local_y = rows // fields
    sign = jnp.where(lax.broadcasted_iota(jnp.int32, (ROWS, width), 1) < block, -1.0, 1.0)

    def times_i(value):
        return sign * pltpu.roll(value, block, 1)

    def coefficients(s0):
        return [weight_ref[a0, 4 * s0 + p] for p in range(4)]

    @pl.when(a1 == 0)
    def _():
        @pl.loop(0, rows // ROWS, unroll=3)
        def _(step):
            at = pl.ds(pl.multiple_of(step * ROWS, ROWS), ROWS)
            z = []
            for s0 in range(4):
                c1, s1, c2, s2 = coefficients(s0)
                first, second = x_ref[s0, at, :], x_ref[s0 + 4, at, :]
                z.append(c1 * first + c2 * second + times_i(s1 * first + s2 * second))
            even, odd = z[0] + z[2], z[0] - z[2]
            total, turned = z[1] + z[3], times_i(z[1] - z[3])
            u_ref[0, at, :] = even + total
            u_ref[1, at, :] = odd + turned
            u_ref[2, at, :] = even - total
            u_ref[3, at, :] = odd - turned

    dot = functools.partial(lax.dot_general, preferred_element_type=jnp.float32)
    plain = (((1,), (0,)), ((), ()))
    flipped = (((1,), (1,)), ((), ()))
    table_high, table_low = high_ref[0], low_ref[0]

    def product(value, dims):
        high, low = split_value(value)
        both = dot(jnp.concatenate([high, low], axis=0), table_high, dims)
        return both[:rows] + both[rows:] + dot(high, table_low, dims)

    physical = product(u_ref[a1], plain).reshape(fields, local_y, width)
    u_ref[a1] = product((physical * fac_ref[0][None]).reshape(rows, width), flipped)

    @pl.when(a1 == 3)
    def _():
        @pl.when(a0 == 0)
        def _():
            y_ref[...] = jnp.zeros_like(y_ref)

        @pl.loop(0, rows // ROWS, unroll=3)
        def _(step):
            at = pl.ds(pl.multiple_of(step * ROWS, ROWS), ROWS)
            even, odd = u_ref[0, at, :] + u_ref[2, at, :], u_ref[0, at, :] - u_ref[2, at, :]
            total, turned = u_ref[1, at, :] + u_ref[3, at, :], times_i(u_ref[1, at, :] - u_ref[3, at, :])
            q = [even + total, odd - turned, even - total, odd + turned]
            for s0 in range(4):
                c1, s1, c2, s2 = coefficients(s0)
                rotated = times_i(q[s0])
                y_ref[s0, at, :] += c1 * q[s0] - s1 * rotated
                y_ref[s0 + 4, at, :] += c2 * q[s0] - s2 * rotated

        @pl.when(a0 == 2)
        def _():
            flow_wave = flow_ref[0]

            @pl.loop(0, local_y // ROWS)
            def _(step):
                def at(field):
                    return pl.ds(pl.multiple_of(field * local_y + step * ROWS, ROWS), ROWS)

                for s in range(BLOCKS):
                    if fields == 1:
                        out_ref[s, at(0), :] = y_ref[s, at(0), :]
                    else:
                        mixed = kz_ref[s : s + 1, :] * y_ref[s, at(0), :] - flow_wave * y_ref[s, at(1), :]
                        out_ref[s, at(0), :] = times_i(mixed)


def spanwise_pass(data, kz_rows, flow_wave, factor, count_z):
    _, rows, width = data.shape
    local_y = factor.shape[1]
    high, low, weights = spanwise_tables(width // 2, count_z)
    whole = pl.BlockSpec(memory_space=pltpu.VMEM)
    scalars = pl.BlockSpec(memory_space=pltpu.SMEM)
    flops = 2 * 2 * 3 * 12 * rows * width * width
    return pl.pallas_call(
        spanwise_kernel,
        grid=(3, 4),
        out_shape=jax.ShapeDtypeStruct((BLOCKS, local_y, width), jnp.float32),
        in_specs=[
            scalars,
            scalars,
            whole,
            whole,
            pl.BlockSpec((1, local_y, width), lambda i, j: (4 * i + j, 0, 0)),
            pl.BlockSpec((1, width, width), lambda i, j: (4 * i + j, 0, 0)),
            pl.BlockSpec((1, width, width), lambda i, j: (4 * i + j, 0, 0)),
        ],
        out_specs=whole,
        scratch_shapes=[
            pltpu.VMEM((4, rows, width), jnp.float32),
            pltpu.VMEM((BLOCKS, rows, width), jnp.float32),
        ],
        compiler_params=pltpu.CompilerParams(vmem_limit_bytes=44 * 2**20),
        cost_estimate=pl.CostEstimate(flops=flops, bytes_accessed=4 * 12 * width * width, transcendentals=0),
        name="spanwise_v" if rows == local_y else "spanwise_omega",
    )(jnp.asarray(weights), flow_wave.reshape(1), data, kz_rows, factor, jnp.asarray(high), jnp.asarray(low))


def gather_maps(forward_map, back_maps):
    share = lax.axis_size("row")
    extent, count_y = forward_map.shape
    if extent % (8 * share):
        forward = lax.all_gather(forward_map, "col", axis=0, tiled=True)
        return forward, lax.all_gather(back_maps, "col", axis=1, tiled=True)
    piece = extent // share
    start = lax.axis_index("row") * piece
    own = [lax.dynamic_slice_in_dim(forward_map, start, piece, 0)[None]]
    own.append(lax.dynamic_slice_in_dim(back_maps, start, piece, 1))
    columns = lax.all_gather(jnp.concatenate(own, axis=0), "col", axis=1, tiled=False)

    def everyone(part):
        rows = lax.all_gather(part, "row", axis=2, tiled=False)
        return rows.reshape(part.shape[0], extent * lax.axis_size("col"), count_y)

    return everyone(columns[:1])[0], [everyone(columns[1:2])[0], everyone(columns[2:])[0]]


def shards(source_v, source_omega, forward_map, back_maps, eigenvalues, penalty):
    _, local_kx, local_kz, count_y = source_v.shape
    assert local_kx == 1
    share = lax.axis_size("row")
    count_kz = local_kz * share
    half_kz = count_kz // 2
    local_y, count_z = penalty.shape
    block = count_kz // BLOCKS
    coarse = count_z // block
    assert coarse == 12 and share % BLOCKS == 0
    flow_wave = 0.5 * lax.axis_index("col").astype(jnp.float32)

    def wave_of(index):
        return jnp.where(index < half_kz, index, index - count_kz).astype(jnp.float32) * 8.0 / half_kz

    span_local = wave_of(lax.axis_index("row") * local_kz + jnp.arange(local_kz, dtype=jnp.int32))
    span = jnp.concatenate([span_local, span_local])[None, :]
    sign = jnp.where(jnp.arange(2 * local_kz) < local_kz, 1.0, -1.0)[None, :]
    scaling = helm_scale(eigenvalues[:, None], flow_wave, span)
    wave_sq = jnp.maximum(flow_wave * flow_wave + span * span, 1.0)

    forward, back = gather_maps(forward_map, back_maps)

    def rows_of(source):
        return source.reshape(2 * local_kz, count_y)

    def turned_rows(source):
        return jnp.concatenate([source[1, 0], source[0, 0]], axis=0)

    def coefficients(rows):
        return jnp.einsum("jn,kn->jk", forward, rows, precision=HIGH) * scaling

    def back_of(which, coeffs):
        return jnp.einsum("yj,jk->yk", back[which], coeffs, precision=HIGH)

    value = back_of(0, coefficients(rows_of(source_v)))
    derivative = back_of(1, coefficients(turned_rows(source_v)))
    vorticity = back_of(0, coefficients(turned_rows(source_omega)))
    along = sign * (span * vorticity - flow_wave * derivative) / wave_sq
    across = -sign * (span * derivative + flow_wave * vorticity) / wave_sq

    def by_owner(field):
        return field.reshape(share, local_y, 2 * local_kz)

    merge = share // BLOCKS

    def sent(*parts):
        fields = jnp.stack([by_owner(part) for part in parts], axis=1)
        data = lax.all_to_all(fields, "row", split_axis=0, concat_axis=0)
        rows = len(parts) * local_y
        if merge > 1:
            data = data.reshape(BLOCKS, merge, rows, 2, local_kz)
            data = jnp.transpose(data, (0, 2, 3, 1, 4))
        return data.reshape(BLOCKS, rows, 2 * block)

    data_v = sent(value)
    data_omega = sent(along, across)

    kz_rows = wave_of(jnp.arange(count_kz, dtype=jnp.int32)).reshape(BLOCKS, block)
    kz_rows = jnp.concatenate([kz_rows, kz_rows], axis=1)
    factor = jnp.transpose(penalty.reshape(local_y, block, coarse), (2, 0, 1))
    factor = factor.reshape(4, 3, local_y, block).transpose(1, 0, 2, 3).reshape(coarse, local_y, block)
    factor = (1.0 / count_z) / (1.0 + factor)
    factor = jnp.concatenate([factor, factor], axis=2)

    def finished(data):
        result = spanwise_pass(data, kz_rows, flow_wave, factor, count_z)
        if merge > 1:
            result = result.reshape(BLOCKS, local_y, 2, merge, local_kz)
            result = jnp.transpose(result, (0, 3, 1, 2, 4))
        result = result.reshape(share, local_y, 2 * local_kz)
        returned = lax.all_to_all(result, "row", split_axis=0, concat_axis=0)
        flat = returned.reshape(count_y, 2 * local_kz)
        return jnp.transpose(flat).reshape(2, 1, local_kz, count_y)

    return finished(data_v), finished(data_omega)


def solution(mesh):
    placed = (
        P(None, "col", "row", None),
        P(None, "col", "row", None),
        P("col", None),
        P(None, "col", None),
        P(),
        P("row", None),
    )
    return jax.shard_map(
        shards,
        mesh=mesh,
        in_specs=placed,
        out_specs=(P(None, "col", "row", None), P(None, "col", "row", None)),
        check_vma=False,
    )
```
